256 devices in a mesh: section: 8 (over y_lo, x), dp: 32 (over y_hi, z, core).
Axes of the slice: x: 4, y: 4 (y_hi: 2, y_lo: 2; y = y_hi * 2 + y_lo), z: 8, core: 2. Of those that a mesh axis runs over, the one named last changes fastest.
Arguments:
- arriving: bfloat16 [8, 32, 128, 8192], P('section', 'dp'), may hold values from -6 to 6
- returning: bfloat16 [8, 32, 128, 8192], P('section', 'dp'), may hold values from -6 to 6
- gain: float32 [8, 8192], P('section'), may hold values from 0.1 to 1.9
- section_down_weight: bfloat16 [8, 128, 8192], P('section', None, 'dp'), may hold values from -0.0625 to 0.0625
- section_up_weight: bfloat16 [8, 128, 8192], P('section', None, 'dp'), may hold values from -0.5 to 0.5
- failed: int32 [8], replicated, may hold values from 0 to 31
- route: int32 [8, 32], replicated, may hold values from 0 to 31, each once within a row
Outputs:
- forward_out: bfloat16 [8, 32, 128, 8192], P('section', 'dp')
- backward_out: bfloat16 [8, 32, 128, 8192], P('section', 'dp')
- rerouted_forward: bfloat16 [8, 128, 8192], P('section', 'dp')
- rerouted_backward: bfloat16 [8, 128, 8192], P('section', 'dp')
- grad_down: float32 [8, 128, 8192], P('section', None, 'dp')
- grad_up: float32 [8, 128, 8192], P('section', None, 'dp')
The draws below stay inside these ranges and needn't reach their ends.
All inputs are finite; a program needn't handle non-finite values.
Results may differ from the reference program's by a relative error of at most 0.005.
Values may be sent and summed in bfloat16 or wider, within the bound.
No kernel may reach another device: no remote copies, remote signals or barrier semaphores. Data moves between devices by JAX's collectives and lax.ppermute only.
A program may use at most 128 MiB of HBM per device.

```python
import jax
import jax.numpy as jnp
from jax import lax

MODEL_WIDTH = 8192
ADAPTER_RANK = 128
ROWS = 128
N_SECTION = 8
N_DP = 32


def with_ends(entries, rng, smallest, top_value):
    spot = [jax.random.randint(jax.random.fold_in(rng, axis), (), 0, length) for axis, length in enumerate(entries.shape)]
    main_axis = entries.shape.index(max(entries.shape))
    neighbour = spot[:main_axis] + [(spot[main_axis] + 1) % entries.shape[main_axis]] + spot[main_axis + 1:]
    return entries.at[tuple(spot)].set(smallest).at[tuple(neighbour)].set(top_value)


def raised(entries, stream_key, source, target, blocks, factor):
    owner, partner = [(jnp.arange(entries.shape[axis_at]) // (entries.shape[axis_at] // blocks)).reshape([-1 if axis == axis_at else 1 for axis in range(entries.ndim)]) for axis_at in (source, target)]
    chosen = jax.random.permutation(stream_key, blocks)[partner]
    strong = (owner == chosen) | (owner == (partner + blocks // 2) % blocks)
    return jnp.where(strong, factor * entries, entries)


def shard_levels(own_key, dims, shards, low, high):
    loudness, own = 1.0, jax.random.fold_in(own_key, 6)
    for axis_at, shards_of in shards:
        draws = jnp.exp(jax.random.uniform(jax.random.fold_in(own, axis_at), (shards_of,), jnp.float32, low / len(shards), high / len(shards)))
        loudness = loudness * jnp.repeat(draws, dims[axis_at] // shards_of).reshape([-1 if axis == axis_at else 1 for axis in range(len(dims))])
    return loudness


def bell_draw(key, dims, deviation, limit, shards=(), kind=jnp.bfloat16):
    array = deviation * jax.random.normal(key, dims, jnp.float32)
    if shards:
        array = array * shard_levels(key, dims, shards, -0.22, 0.18)
    return jnp.clip(array, -limit, limit).astype(kind)


def bell_draw_with(rng, shape, deviation, most, cuts, heavy, held_as=jnp.bfloat16):
    entries = deviation * jax.random.normal(rng, shape, jnp.float32)
    if cuts:
        entries = entries * shard_levels(rng, shape, cuts, -0.22, 0.18)
    return jnp.clip(raised(entries, jax.random.fold_in(rng, 3), *heavy), -most, most).astype(held_as)


def setup_inputs(seed: int = 0) -> dict:
    streams_of = jax.random.split(jax.random.key(seed), 8)
    return {
        "arriving": bell_draw(streams_of[0], (N_SECTION, N_DP, ROWS, MODEL_WIDTH), 1.0, 6.0, ((0, 8), (1, 32))),
        "returning": bell_draw_with(streams_of[1], (N_SECTION, N_DP, ROWS, MODEL_WIDTH), 1.0, 6.0, ((0, 8), (1, 32)), (1, 3, 32, 2.75)),
        "gain": jnp.clip(1.0 + 0.18 * jax.random.normal(streams_of[2], (N_SECTION, MODEL_WIDTH), jnp.float32), 0.1, 1.9),
        "section_down_weight": bell_draw(streams_of[3], (N_SECTION, ADAPTER_RANK, MODEL_WIDTH), MODEL_WIDTH ** -0.5, 0.0625, ((0, 8), (2, 32))),
        "section_up_weight": bell_draw(streams_of[4], (N_SECTION, ADAPTER_RANK, MODEL_WIDTH), ADAPTER_RANK ** -0.5, 0.5, ((0, 8), (2, 32))),
        "failed": with_ends(jax.random.randint(streams_of[5], (N_SECTION,), 0, N_DP), jax.random.fold_in(streams_of[5], 1), 0, N_DP - 1).astype(jnp.int32),
        "route": jax.vmap(lambda own: jax.random.permutation(own, N_DP))(jax.random.split(streams_of[6], N_SECTION)).reshape((N_SECTION, N_DP)).astype(jnp.int32),
    }


eps = 1e-05

def layer(acts, grads, scale, down_weight, up_weight):
    act32 = acts.astype(jnp.float32)

    def normalize(rows):
        inv = lax.rsqrt(lax.optimization_barrier(jnp.mean(rows * rows, axis=-1, keepdims=True)) + eps)
        return rows * inv * scale
    normed32, pull = jax.vjp(normalize, act32)
    normed = normed32.astype(jnp.bfloat16)
    low = lax.dot_general(normed, down_weight, (((1,), (1,)), ((), ())), preferred_element_type=jnp.float32).astype(jnp.bfloat16)
    lifted = jnp.dot(low, up_weight, preferred_element_type=jnp.float32)
    outputs = (act32 + lifted).astype(jnp.bfloat16)
    back_low = lax.dot_general(grads, up_weight, (((1,), (1,)), ((), ())), preferred_element_type=jnp.float32).astype(jnp.bfloat16)
    back_norm = jnp.dot(back_low, down_weight, preferred_element_type=jnp.float32)
    back_x = (grads.astype(jnp.float32) + pull(back_norm)[0]).astype(jnp.bfloat16)
    grad_a = lax.dot_general(back_low, normed, (((0,), (0,)), ((), ())), preferred_element_type=jnp.float32)
    grad_b = lax.dot_general(low, grads, (((0,), (0,)), ((), ())), preferred_element_type=jnp.float32)
    return (outputs, back_x, grad_a, grad_b)

def reference(arriving, returning, gain, section_down_weight, section_up_weight, failed, route):
    ranks = jnp.arange(N_DP, dtype=jnp.int32)
    share = ROWS // N_DP

    def one(update_step):
        before = ((update_step - 1) % N_SECTION).astype(jnp.int32)
        after = ((update_step + 1) % N_SECTION).astype(jnp.int32)
        acts = lax.dynamic_index_in_dim(arriving, before, 0, keepdims=False).reshape(N_DP * ROWS, MODEL_WIDTH)
        grads = lax.dynamic_index_in_dim(returning, after, 0, keepdims=False).reshape(N_DP * ROWS, MODEL_WIDTH)
        scale = lax.dynamic_index_in_dim(gain, update_step, 0, keepdims=False)
        down_weight = lax.dynamic_index_in_dim(section_down_weight, update_step, 0, keepdims=False)
        up_weight = lax.dynamic_index_in_dim(section_up_weight, update_step, 0, keepdims=False)
        outputs, back_x, grad_a, grad_b = layer(acts, grads, scale, down_weight, up_weight)
        lost = lax.dynamic_index_in_dim(failed, update_step, 0, keepdims=False).astype(jnp.int32)
        order = lax.dynamic_index_in_dim(route, update_step, 0, keepdims=False).astype(jnp.int32)
        keeps = (ranks != lost)[:, None, None]

        def place(block):
            block = block.reshape(N_DP, ROWS, MODEL_WIDTH)
            own = jnp.where(keeps, block, jnp.zeros_like(block))
            taken = lax.dynamic_index_in_dim(block, lost, 0, keepdims=False).reshape(N_DP, share, MODEL_WIDTH)
            moved = jnp.take(taken, order, axis=0).reshape(ROWS, MODEL_WIDTH)
            return (own, moved)
        own_f, moved_f = place(outputs)
        own_b, moved_b = place(back_x)
        return (own_f, own_b, moved_f, moved_b, grad_a / N_DP, grad_b / N_DP)
    results = lax.map(one, jnp.arange(N_SECTION, dtype=jnp.int32))
    return (results[0], results[1], results[2], results[3], results[4], results[5])
```

```python
import jax
import jax.numpy as jnp
from jax import lax
from jax.experimental import pallas as pl
from jax.experimental.pallas import tpu as pltpu
from jax.sharding import PartitionSpec as P

eps = 1e-05
N_Z = 8
N_DP = 32
BLOCK = 256
F32 = jnp.float32
BF16 = jnp.bfloat16


def place(y, z, c):
    return (y * N_Z + z) * 2 + c


PLACES = [(y, z, c) for y in range(2) for z in range(N_Z) for c in range(2)]
TO_CORE = [(place(y, z, c), place(y, z, 1 - c)) for y, z, c in PLACES]
TO_Y = [(place(y, z, c), place(1 - y, z, c)) for y, z, c in PLACES]
TO_UP = [(place(y, z, c), place(y, (z + 1) % N_Z, c)) for y, z, c in PLACES]
TO_DOWN = [(place(y, z, c), place(y, (z - 1) % N_Z, c)) for y, z, c in PLACES]
Z_GROUPS = [[place(y, z, c) for z in range(N_Z)] for y in range(2) for c in range(2)]


def over_dp(block, pairs):
    return lax.ppermute(block, "dp", pairs)


def over_section(block, distance):
    n = lax.axis_size("section")
    return lax.ppermute(block, "section", [(i, (i + distance) % n) for i in range(n)])


def ring_sum(own, half, narrow):
    first, second = half(own(4))
    up, down = over_dp(narrow(first), TO_UP), over_dp(narrow(second), TO_DOWN)
    f0, f1 = half(own(3))
    g0, g1 = half(own(5))
    up = jnp.concatenate([f0 + up.astype(F32), f1], axis=0)
    down = jnp.concatenate([g0, g1 + down.astype(F32)], axis=0)
    up, down = over_dp(narrow(up), TO_UP), over_dp(narrow(down), TO_DOWN)
    for k in (2, 1):
        up = over_dp(narrow(own(k) + up.astype(F32)), TO_UP)
        down = over_dp(narrow(own(8 - k) + down.astype(F32)), TO_DOWN)
    return own(0) + up.astype(F32) + down.astype(F32)


def terms_kernel(
    at, x_ref, g_ref, gain_ref, w0_ref, w1_ref,
    keep_d, keep_u, send_d, send_u, low_ref, back_ref, inv_ref, dot_ref, normed,
):
    rows, width = x_ref.shape
    z = at[32]

    def square(i, total):
        part = x_ref[:, pl.ds(pl.multiple_of(i * 512, 512), 512)].astype(F32)
        part = part * part
        return total + (part[:, :128] + part[:, 128:256]) + (part[:, 256:384] + part[:, 384:])

    total = lax.fori_loop(0, width // 512, square, jnp.zeros((rows, 128), F32))
    inv = lax.rsqrt(jnp.sum(total, axis=1, keepdims=True) * (1.0 / width) + eps)
    trans = (((1,), (1,)), ((), ()))

    def lows(k, sums):
        low, back = sums
        spot = lax.rem(z + k, N_Z)
        for c, w_ref in enumerate((w0_ref, w1_ref)):
            for y in range(2):
                off = pl.multiple_of(at[(c * N_Z + k) * 2 + y], BLOCK)
                part = x_ref[:, pl.ds(off, BLOCK)].astype(F32)
                norm = (part * inv * gain_ref[:, pl.ds(off, BLOCK)]).astype(BF16)
                normed[(c * N_Z + k) * 2 + y] = norm
                low += lax.dot_general(norm, w_ref[spot, y, 0], trans, preferred_element_type=F32)
                back += lax.dot_general(
                    g_ref[:, pl.ds(off, BLOCK)], w_ref[spot, y, 1], trans, preferred_element_type=F32
                )
        return low, back

    zero = jnp.zeros((rows, low_ref.shape[1]), F32)
    low, back = lax.fori_loop(0, N_Z, lows, (zero, zero))
    low16, back16 = low.astype(BF16), back.astype(BF16)
    low_ref[...] = low16
    back_ref[...] = back16
    inv_ref[...] = jnp.broadcast_to(inv, inv_ref.shape)
    dots = jnp.sum(back16.astype(F32) * low, axis=1, keepdims=True)
    dot_ref[...] = jnp.broadcast_to(dots, dot_ref.shape)
    low_t, back_t = low16.T, back16.T

    def terms(k, carry):
        for c in range(2):
            for y in range(2):
                spot = (c * N_Z + k) * 2 + y
                off = pl.multiple_of(at[spot], BLOCK)
                down = jnp.dot(back_t, normed[spot], preferred_element_type=F32)
                up = jnp.dot(low_t, g_ref[:, pl.ds(off, BLOCK)], preferred_element_type=F32)
                if c == 0:
                    keep_d[k, y] = down
                    keep_u[k, y] = up
                else:
                    send_d[k, y] = down.astype(BF16)
                    send_u[k, y] = up.astype(BF16)
        return carry

    lax.fori_loop(0, N_Z, terms, 0)


def outputs_kernel(
    at, x_ref, g_ref, gain_ref, w0_ref, w1_ref, low_ref, back_ref, inv_ref, dot_ref, xe_ref, ge_ref,
    fwd, bwd, fwd_e, bwd_e,
):
    rows, width = x_ref.shape
    z = at[32]
    keeps = at[33] == 1
    trans = (((1,), (1,)), ((), ()))
    extra = xe_ref.shape[0]

    def square(i, total):
        part = xe_ref[:, pl.ds(pl.multiple_of(i * 128, 128), 128)].astype(F32)
        return total + part * part

    total = lax.fori_loop(0, width // 128, square, jnp.zeros((extra, 128), F32))
    inv_e = lax.rsqrt(jnp.sum(total, axis=1, keepdims=True) * (1.0 / width) + eps)

    def lows(k, sums):
        low, back = sums
        spot = lax.rem(z + k, N_Z)
        for c, w_ref in enumerate((w0_ref, w1_ref)):
            for y in range(2):
                off = pl.multiple_of(at[(c * N_Z + k) * 2 + y], BLOCK)
                part = xe_ref[:, pl.ds(off, BLOCK)].astype(F32)
                norm = (part * inv_e * gain_ref[:, pl.ds(off, BLOCK)]).astype(BF16)
                low += lax.dot_general(norm, w_ref[spot, y, 0], trans, preferred_element_type=F32)
                back += lax.dot_general(
                    ge_ref[:, pl.ds(off, BLOCK)], w_ref[spot, y, 1], trans, preferred_element_type=F32
                )
        return low, back

    zero = jnp.zeros((extra, low_ref.shape[1]), F32)
    low_e, back_e = lax.fori_loop(0, N_Z, lows, (zero, zero))
    low_e16, back_e16 = low_e.astype(BF16), back_e.astype(BF16)
    dots_e = jnp.sum(back_e16.astype(F32) * low_e, axis=1, keepdims=True)
    low = jnp.concatenate([low_ref[...], low_e16], axis=0)
    back = jnp.concatenate([back_ref[...], back_e16], axis=0)
    inv = inv_ref[:, :1]
    slope = inv * inv * dot_ref[:, :1] * (1.0 / width)
    slope_e = inv_e * inv_e * dots_e * (1.0 / width)

    def outs(k, carry):
        spot = lax.rem(z + k, N_Z)
        for c, w_ref in enumerate((w0_ref, w1_ref)):
            for y in range(2):
                off = pl.multiple_of(at[(c * N_Z + k) * 2 + y], BLOCK)
                here = pl.ds(off, BLOCK)
                scale = gain_ref[:, here]
                lifted = jnp.dot(low, w_ref[spot, y, 1], preferred_element_type=F32)
                pulled = jnp.dot(back, w_ref[spot, y, 0], preferred_element_type=F32) * scale
                part = x_ref[:, here].astype(F32)
                part_e = xe_ref[:, here].astype(F32)
                out = (part + lifted[:rows]).astype(BF16)
                grad = g_ref[:, here].astype(F32) + (pulled[:rows] * inv - part * slope)
                fwd[:, here] = jnp.where(keeps, out, jnp.zeros_like(out))
                grad = grad.astype(BF16)
                bwd[:, here] = jnp.where(keeps, grad, jnp.zeros_like(grad))
                fwd_e[:, here] = (part_e + lifted[rows:]).astype(BF16)
                grad_e = ge_ref[:, here].astype(F32) + (pulled[rows:] * inv_e - part_e * slope_e)
                bwd_e[:, here] = grad_e.astype(BF16)
        return carry

    lax.fori_loop(0, N_Z, outs, 0)


def picks(route, lost, rank, y, z, c, c_rel, slot, count):
    share = count // N_DP
    row = jnp.arange(count)
    k, q = row // 16, row % 16
    y_to = jnp.where(q >= 8, 1 - y, y)
    c_to = c if c_rel == 0 else 1 - c
    to = place(y_to, (z + k) % N_Z, c_to)
    source = route[to] * share + q % share
    used = (rank == lost) & ((q // 4) % 2 == slot)
    return ((source[:, None] == jnp.arange(count)[None, :]) & used[:, None]).astype(BF16)


def body(arriving, returning, gain, section_down_weight, section_up_weight, failed, route):
    section = lax.axis_index("section")
    sections = lax.axis_size("section")
    rank = lax.axis_index("dp")
    y, z, c = rank // 16, (rank // 2) % N_Z, rank % 2
    count, width = arriving.shape[2], arriving.shape[3]
    depth = section_down_weight.shape[1]
    share = count // N_DP

    inbound = over_section(arriving, 1)[0, 0]
    upstream = over_section(returning, -1)[0, 0]

    shard = jnp.concatenate([section_down_weight, section_up_weight], axis=0)
    both = jnp.stack([shard, over_dp(shard, TO_Y)], axis=0)
    mine = lax.all_gather(both, "dp", axis=0, axis_index_groups=Z_GROUPS, tiled=False)
    theirs = over_dp(mine, TO_CORE)

    here_x, here_g = arriving[0, 0], returning[0, 0]
    after, before = (section + 1) % sections, (section - 1) % sections
    moved = []
    for c_rel in range(2):
        px = picks(route[after], failed[after], rank, y, z, c, c_rel, 0, count)
        pg = picks(route[before], failed[before], rank, y, z, c, c_rel, 1, count)
        rows = jnp.dot(px, here_x, preferred_element_type=F32) + jnp.dot(
            pg, here_g, preferred_element_type=F32
        )
        moved.append(rows.astype(BF16).reshape(N_Z, 16, width))
    crossed = over_dp(moved[1], TO_CORE)
    rows = ring_sum(
        lambda k: moved[0][k].astype(F32) + crossed[k].astype(F32),
        lambda v: (v[:8], v[8:]),
        lambda v: v.astype(BF16),
    ).astype(BF16)
    rows = rows[:8] + over_dp(rows[8:], TO_Y)
    extra_x = over_section(rows[:share], 1)
    extra_g = over_section(rows[share : 2 * share], -1)
    pad = ((0, 16 - share), (0, 0))
    extra_x, extra_g = jnp.pad(extra_x, pad), jnp.pad(extra_g, pad)

    offsets = [
        place(y if yr == 0 else 1 - y, (z + k) % N_Z, c if cr == 0 else 1 - c) * BLOCK
        for cr in range(2)
        for k in range(N_Z)
        for yr in range(2)
    ]
    at = jnp.stack(offsets + [z, (rank != failed[section]).astype(jnp.int32)]).astype(jnp.int32)
    smem = pl.BlockSpec(memory_space=pltpu.SMEM)
    vmem = pl.BlockSpec(memory_space=pltpu.VMEM)
    chunk = (N_Z, 2, depth, BLOCK)
    stat = jax.ShapeDtypeStruct((count, 128), F32)
    small = jax.ShapeDtypeStruct((count, depth), BF16)
    keep_d, keep_u, send_d, send_u, low, back, inv, dots = pl.pallas_call(
        terms_kernel,
        out_shape=[
            jax.ShapeDtypeStruct(chunk, F32),
            jax.ShapeDtypeStruct(chunk, F32),
            jax.ShapeDtypeStruct(chunk, BF16),
            jax.ShapeDtypeStruct(chunk, BF16),
            small,
            small,
            stat,
            stat,
        ],
        in_specs=[smem] + [vmem] * 5,
        out_specs=[vmem] * 8,
        scratch_shapes=[pltpu.VMEM((32, count, BLOCK), BF16)],
        compiler_params=pltpu.CompilerParams(vmem_limit_bytes=40 * 2**20),
        cost_estimate=pl.CostEstimate(
            flops=8 * count * width * depth, bytes_accessed=16 * 2**20, transcendentals=0
        ),
        name="terms",
    )(at, inbound, upstream, gain, mine, theirs)

    def reduced(keep, send):
        crossed = over_dp(send, TO_CORE)
        total = ring_sum(
            lambda k: keep[k] + crossed[k].astype(F32),
            lambda v: (v[:1], v[1:]),
            lambda v: v.astype(BF16),
        )
        other = over_dp(total[1].astype(BF16), TO_Y)
        return ((total[0] + other.astype(F32)) * (1.0 / N_DP))[None]

    grad_up = reduced(keep_u, send_u)
    grad_down = reduced(keep_d, send_d)

    wide = jax.ShapeDtypeStruct((count, width), BF16)
    thin = jax.ShapeDtypeStruct((16, width), BF16)
    forward_out, backward_out, rerouted_f, rerouted_b = pl.pallas_call(
        outputs_kernel,
        out_shape=[wide, wide, thin, thin],
        in_specs=[smem] + [vmem] * 11,
        out_specs=[vmem] * 4,
        compiler_params=pltpu.CompilerParams(vmem_limit_bytes=40 * 2**20),
        cost_estimate=pl.CostEstimate(
            flops=5 * count * width * depth, bytes_accessed=14 * 2**20, transcendentals=0
        ),
        name="outputs",
    )(at, inbound, upstream, gain, mine, theirs, low, back, inv, dots, extra_x, extra_g)
    return (
        forward_out[None, None],
        backward_out[None, None],
        rerouted_f[None, :share],
        rerouted_b[None, :share],
        grad_down,
        grad_up,
    )


def solution(mesh):
    return jax.shard_map(
        body,
        mesh=mesh,
        in_specs=(
            P("section", "dp", None, None),
            P("section", "dp", None, None),
            P("section", None),
            P("section", None, "dp"),
            P("section", None, "dp"),
            P(),
            P(),
        ),
        out_specs=(
            P("section", "dp", None, None),
            P("section", "dp", None, None),
            P("section", "dp", None),
            P("section", "dp", None),
            P("section", None, "dp"),
            P("section", None, "dp"),
        ),
        check_vma=False,
    )
```

```python
import jax
import jax.numpy as jnp
from jax import lax
from jax.experimental import pallas as pl
from jax.experimental.pallas import tpu as pltpu
from jax.sharding import PartitionSpec as P

eps = 1e-05
N_Z = 8
N_DP = 32
BLOCK = 256
F32 = jnp.float32
BF16 = jnp.bfloat16


def place(y, z, c):
    return (y * N_Z + z) * 2 + c


PLACES = [(y, z, c) for y in range(2) for z in range(N_Z) for c in range(2)]
TO_CORE = [(place(y, z, c), place(y, z, 1 - c)) for y, z, c in PLACES]
TO_Y = [(place(y, z, c), place(1 - y, z, c)) for y, z, c in PLACES]
TO_UP = [(place(y, z, c), place(y, (z + 1) % N_Z, c)) for y, z, c in PLACES]
TO_DOWN = [(place(y, z, c), place(y, (z - 1) % N_Z, c)) for y, z, c in PLACES]
Z_GROUPS = [[place(y, z, c) for z in range(N_Z)] for y in range(2) for c in range(2)]


def over_dp(block, pairs):
    return lax.ppermute(block, "dp", pairs)


def over_section(block, distance):
    n = lax.axis_size("section")
    return lax.ppermute(block, "section", [(i, (i + distance) % n) for i in range(n)])


def over_both(block, distance, across):
    n = lax.axis_size("section")
    pairs = [
        (i * N_DP + place(y, z, c), (i + distance) % n * N_DP + place(y ^ across, z, c))
        for i in range(n)
        for y, z, c in PLACES
    ]
    return lax.ppermute(block, ("section", "dp"), pairs)


SLOTS = (4, 3, 5, 2, 6, 1, 7, 0)
N_FIRST = 3


def columns_of(refs, at, c, k, y):
    return refs[c].at[lax.rem(at[32] + k, N_Z), y]


def spot_of(c, k, y):
    return (c * N_Z + k) * 2 + y


def wide(ref):
    return ref[...].astype(F32)


def open_kernel(keep, crossed, up, down):
    total = keep[0] + wide(crossed)[0]
    up[...] = total[:1].astype(BF16)
    down[...] = total[1:].astype(BF16)


def fold_kernel(token, keep_up, keep_down, cross_up, cross_down, got_up, got_down, up, down):
    top = keep_up[0] + wide(cross_up)[0]
    low = keep_down[0] + wide(cross_down)[0]
    if got_up.shape[0] == 1:
        up[0] = (top[0] + wide(got_up)[0]).astype(BF16)
        up[1] = top[1].astype(BF16)
        down[0] = low[0].astype(BF16)
        down[1] = (low[1] + wide(got_down)[0]).astype(BF16)
    else:
        up[...] = (top + wide(got_up)).astype(BF16)
        down[...] = (low + wide(got_down)).astype(BF16)


def close_kernel(keep, crossed, got_up, got_down, own, other):
    total = (keep[0] + wide(crossed)[0]) + (wide(got_up) + wide(got_down))
    own[...] = total[0]
    other[...] = total[1].astype(BF16)


def finish_kernel(own, got, grad_down, grad_up):
    total = (own[...] + wide(got)) * (1.0 / N_DP)
    grad_down[0] = total[0]
    grad_up[0] = total[1]


def square_sums(x_ref):
    rows, width = x_ref.shape

    def square(i, total):
        part = x_ref[:, pl.ds(pl.multiple_of(i * 512, 512), 512)].astype(F32)
        part = part * part
        return total + ((part[:, :128] + part[:, 128:256]) + (part[:, 256:384] + part[:, 384:]))

    total = lax.fori_loop(0, width // 512, square, jnp.zeros((rows, 128), F32))
    return lax.rsqrt(jnp.sum(total, axis=1, keepdims=True) * (1.0 / width) + eps)


def scale_kernel(x_ref, g_ref, inv_ref):
    inv_ref[...] = jnp.broadcast_to(square_sums(x_ref), inv_ref.shape)


def add_kernel(token, a_ref, b_ref, out_ref):
    out_ref[...] = a_ref[...] + b_ref[...]


def lows_of(at, x_ref, g_ref, gain_ref, w_refs, inv, normed):
    trans = (((1,), (1,)), ((), ()))
    low = back = None
    for c in range(2):
        for k in range(N_Z):
            for y in range(2):
                spot = spot_of(c, k, y)
                here = pl.ds(pl.multiple_of(at[spot], BLOCK), BLOCK)
                norm = (x_ref[:, here].astype(F32) * inv * gain_ref[:, here]).astype(BF16)
                if normed is not None:
                    normed[spot] = norm
                w = columns_of(w_refs, at, c, k, y)
                one = lax.dot_general(norm, w[0], trans, preferred_element_type=F32)
                two = lax.dot_general(g_ref[:, here], w[1], trans, preferred_element_type=F32)
                low, back = (one, two) if low is None else (low + one, back + two)
    return low, back


def terms_kernel(at, x_ref, g_ref, gain_ref, *refs):
    w_refs = refs[:2]
    inv_ref, keep_ref, first_ref, second_ref, low_ref, back_ref, dot_ref, normed = refs[2:]
    inv = inv_ref[:, :1]
    low, back = lows_of(at, x_ref, g_ref, gain_ref, w_refs, inv, normed)
    low16, back16 = low.astype(BF16), back.astype(BF16)
    low_ref[...] = low16
    back_ref[...] = back16
    dots = jnp.sum(back16.astype(F32) * low, axis=1, keepdims=True)
    dot_ref[...] = jnp.broadcast_to(dots, dot_ref.shape)
    low_t, back_t = low16.T, back16.T

    def term(spot):
        here = pl.ds(pl.multiple_of(at[spot], BLOCK), BLOCK)
        down = jnp.dot(back_t, normed[spot], preferred_element_type=F32)
        up = jnp.dot(low_t, g_ref[:, here], preferred_element_type=F32)
        return down, up

    for i, k in enumerate(SLOTS):
        out_ref, j = (first_ref, i) if i < N_FIRST else (second_ref, i - N_FIRST)
        for y in range(2):
            for which, value in enumerate(term(spot_of(1, k, y))):
                out_ref[j, y, which] = value.astype(BF16)
            for which, value in enumerate(term(spot_of(0, k, y))):
                keep_ref[i, y, which] = value


def write_outputs(at, x_ref, g_ref, gain_ref, w_refs, low, back, inv, slope, fwd, bwd, keeps=None):
    for c in range(2):
        for k in range(N_Z):
            for y in range(2):
                here = pl.ds(pl.multiple_of(at[spot_of(c, k, y)], BLOCK), BLOCK)
                w = columns_of(w_refs, at, c, k, y)
                lifted = jnp.dot(low, w[1], preferred_element_type=F32)
                pulled = jnp.dot(back, w[0], preferred_element_type=F32)
                part = x_ref[:, here].astype(F32)
                out = (part + lifted).astype(BF16)
                grad = g_ref[:, here].astype(F32) + (pulled * gain_ref[:, here] * inv - part * slope)
                grad = grad.astype(BF16)
                if keeps is not None:
                    out = jnp.where(keeps, out, jnp.zeros_like(out))
                    grad = jnp.where(keeps, grad, jnp.zeros_like(grad))
                fwd[:, here] = out
                bwd[:, here] = grad


def outputs_kernel(token, at, x_ref, g_ref, gain_ref, *refs):
    w_refs = refs[:2]
    low_ref, back_ref, inv_ref, dot_ref, fwd, bwd = refs[2:]
    inv = inv_ref[:, :1]
    slope = inv * inv * dot_ref[:, :1] * (1.0 / x_ref.shape[1])
    write_outputs(
        at, x_ref, g_ref, gain_ref, w_refs, low_ref[...], back_ref[...], inv, slope, fwd, bwd,
        at[33] == 1,
    )


def extras_kernel(token, at, x_ref, g_ref, gain_ref, *refs):
    w_refs = refs[:2]
    fwd, bwd = refs[2:]
    inv = square_sums(x_ref)
    low, back = lows_of(at, x_ref, g_ref, gain_ref, w_refs, inv, None)
    low16, back16 = low.astype(BF16), back.astype(BF16)
    dots = jnp.sum(back16.astype(F32) * low, axis=1, keepdims=True)
    slope = inv * inv * dots * (1.0 / x_ref.shape[1])
    write_outputs(at, x_ref, g_ref, gain_ref, w_refs, low16, back16, inv, slope, fwd, bwd)


def picks_kernel(at, after, before, x_ref, g_ref, keep_ref, send_ref, pick):
    count = x_ref.shape[0]
    share = count // N_DP
    y, c = at[35], at[36]

    @pl.when(pl.program_id(0) == 0)
    def _():
        column = lax.broadcasted_iota(jnp.int32, (8, count), 1)
        line = lax.broadcasted_iota(jnp.int32, (8, count), 0)
        has_x, has_g = at[37].astype(F32), at[38].astype(F32)
        for c_rel in range(2):
            parts_x, parts_g = [], []
            for k in range(N_Z):
                for y_to in (y, 1 - y):
                    to = place(y_to, k, c if c_rel == 0 else 1 - c)
                    hit_x = (column == after[to] * share + line) & (line < share)
                    hit_g = (column == before[to] * share + line - share) & (line >= share)
                    parts_x.append(jnp.where(hit_x, has_x, 0.0))
                    parts_g.append(jnp.where(hit_g, has_g, 0.0))
            pick[c_rel, 0] = jnp.concatenate(parts_x, axis=0).astype(BF16)
            pick[c_rel, 1] = jnp.concatenate(parts_g, axis=0).astype(BF16)

    for c_rel, out_ref in ((0, keep_ref), (1, send_ref)):
        moved = jnp.dot(pick[c_rel, 0], x_ref[...], preferred_element_type=F32)
        moved += jnp.dot(pick[c_rel, 1], g_ref[...], preferred_element_type=F32)
        out_ref[...] = moved.astype(BF16)


def body(arriving, returning, gain, section_down_weight, section_up_weight, failed, route):
    section = lax.axis_index("section")
    sections = lax.axis_size("section")
    rank = lax.axis_index("dp")
    y, z, c = rank // 16, (rank // 2) % N_Z, rank % 2
    count, width = arriving.shape[2], arriving.shape[3]
    depth = section_down_weight.shape[1]
    share = count // N_DP

    inbound = over_section(arriving, 1)[0, 0]
    upstream = over_section(returning, -1)[0, 0]

    here_x, here_g = arriving[0, 0], returning[0, 0]
    after, before = (section + 1) % sections, (section - 1) % sections
    offsets = [
        place(y if yr == 0 else 1 - y, (z + k) % N_Z, c if cr == 0 else 1 - c) * BLOCK
        for cr in range(2)
        for k in range(N_Z)
        for yr in range(2)
    ]
    flags = [z, rank != failed[section], 0, y, c, rank == failed[after], rank == failed[before]]
    at = jnp.stack([jnp.asarray(v, jnp.int32) for v in offsets + flags])
    smem = pl.BlockSpec(memory_space=pltpu.SMEM)
    vmem = pl.BlockSpec(memory_space=pltpu.VMEM)
    whole = jax.ShapeDtypeStruct((count, width), BF16)
    params = pltpu.CompilerParams(vmem_limit_bytes=28 * 2**20)
    step = 1024
    block = pl.BlockSpec((count, step), lambda i: (0, i))
    moved = pl.pallas_call(
        picks_kernel,
        grid=(width // step,),
        out_shape=[whole, whole],
        in_specs=[smem] * 3 + [block] * 2,
        out_specs=[block] * 2,
        scratch_shapes=[pltpu.VMEM((2, 2, count, count), BF16)],
        compiler_params=params,
        cost_estimate=pl.CostEstimate(
            flops=4 * count * width * count, bytes_accessed=8 * 2**20, transcendentals=0
        ),
        name="picks",
    )(at, route[after], route[before], here_x, here_g)
    crossed = over_dp(moved[1], TO_CORE)
    stat = jax.ShapeDtypeStruct((count, 128), F32)
    free = pl.BlockSpec(memory_space=pl.ANY)
    inv = pl.pallas_call(
        scale_kernel,
        out_shape=stat,
        in_specs=[vmem, free],
        out_specs=vmem,
        compiler_params=params,
        cost_estimate=pl.CostEstimate(
            flops=2 * count * width, bytes_accessed=40 * 2**20, transcendentals=0
        ),
        name="scale",
    )(inbound, upstream)
    rows = pl.pallas_call(
        add_kernel,
        grid=(4,),
        out_shape=whole,
        in_specs=[free] + [pl.BlockSpec((count // 4, width), lambda i: (i, 0))] * 2,
        out_specs=pl.BlockSpec((count // 4, width), lambda i: (i, 0)),
        compiler_params=params,
        cost_estimate=pl.CostEstimate(
            flops=count * width, bytes_accessed=6 * 2**20, transcendentals=0
        ),
        name="add",
    )(inv, moved[0], crossed)
    rows = lax.psum_scatter(
        rows, "dp", scatter_dimension=0, axis_index_groups=Z_GROUPS, tiled=True
    )

    shard = jnp.concatenate([section_down_weight, section_up_weight], axis=0)
    chunk = (2, 2, depth, BLOCK)
    both = jnp.stack([shard, over_dp(shard, TO_Y)], axis=0)
    mine = lax.all_gather(both, "dp", axis=0, axis_index_groups=Z_GROUPS, tiled=False)
    weights = [mine, over_dp(mine, TO_CORE)]

    small = jax.ShapeDtypeStruct((count, depth), BF16)
    keep, first, second, low, back, dots = pl.pallas_call(
        terms_kernel,
        out_shape=[
            jax.ShapeDtypeStruct((N_Z, *chunk), F32),
            jax.ShapeDtypeStruct((N_FIRST, *chunk), BF16),
            jax.ShapeDtypeStruct((N_Z - N_FIRST, *chunk), BF16),
            small,
            small,
            stat,
        ],
        in_specs=[smem] + [vmem] * 6,
        out_specs=[vmem] * 6,
        scratch_shapes=[pltpu.VMEM((32, count, BLOCK), BF16)],
        compiler_params=params,
        cost_estimate=pl.CostEstimate(
            flops=8 * count * width * depth, bytes_accessed=16 * 2**20, transcendentals=0
        ),
        name="terms",
    )(at, inbound, upstream, gain, *weights, inv)
    first, second = over_dp(first, TO_CORE), over_dp(second, TO_CORE)

    def slot(i):
        return pl.BlockSpec((1, *chunk), lambda j: (i, 0, 0, 0, 0))

    def all_of(shape):
        return pl.BlockSpec(shape, lambda j: (0,) * len(shape))

    half = jax.ShapeDtypeStruct((1, *chunk[1:]), BF16)
    full = jax.ShapeDtypeStruct(chunk, BF16)
    quick = pl.CostEstimate(flops=2**18, bytes_accessed=2**20, transcendentals=0)
    up, down = pl.pallas_call(
        open_kernel,
        grid=(1,),
        out_shape=[half, half],
        in_specs=[slot(0), slot(0)],
        out_specs=[all_of(half.shape)] * 2,
        compiler_params=params,
        cost_estimate=quick,
        name="open",
    )(keep, first)

    def fold(token, i, crossed, j, up, down):
        return pl.pallas_call(
            fold_kernel,
            grid=(1,),
            out_shape=[full, full],
            in_specs=[free, slot(i), slot(i + 1), slot(j), slot(j + 1)] + [all_of(up.shape)] * 2,
            out_specs=[all_of(full.shape)] * 2,
            compiler_params=params,
        cost_estimate=quick,
            name="fold",
        )(token, keep, keep, crossed, crossed, up, down)

    forward_out, backward_out = pl.pallas_call(
        outputs_kernel,
        out_shape=[whole, whole],
        in_specs=[free, smem] + [vmem] * 9,
        out_specs=[vmem] * 2,
        compiler_params=params,
        cost_estimate=pl.CostEstimate(
            flops=4 * count * width * depth, bytes_accessed=14 * 2**20, transcendentals=0
        ),
        name="outputs",
    )(first, at, inbound, upstream, gain, *weights, low, back, inv, dots)

    up, down = over_dp(up, TO_UP), over_dp(down, TO_DOWN)
    up, down = fold(forward_out, 1, first, 1, up, down)
    up, down = over_dp(up, TO_UP), over_dp(down, TO_DOWN)
    up, down = fold(up, 3, second, 0, up, down)
    up, down = over_dp(up, TO_UP), over_dp(down, TO_DOWN)
    up, down = fold(up, 5, second, 2, up, down)
    rows = rows + up[0, 0, :1, :1] * 0
    extras = []
    for i, distance in ((0, 1), (1, -1)):
        near = over_both(rows[i * share : (i + 1) * share], distance, 0)
        far = over_both(rows[8 + i * share : 8 + (i + 1) * share], distance, 1)
        extras.append(jnp.pad(near + far, ((0, 16 - share), (0, 0))))
    up, down = over_dp(up, TO_UP), over_dp(down, TO_DOWN)
    own, other = pl.pallas_call(
        close_kernel,
        grid=(1,),
        out_shape=[
            jax.ShapeDtypeStruct(chunk[1:], F32),
            jax.ShapeDtypeStruct(chunk[1:], BF16),
        ],
        in_specs=[slot(7), slot(4)] + [all_of(chunk)] * 2,
        out_specs=[all_of(chunk[1:])] * 2,
        compiler_params=params,
        cost_estimate=quick,
        name="close",
    )(keep, second, up, down)
    other = over_dp(other, TO_Y)
    thin = jax.ShapeDtypeStruct((16, width), BF16)
    rerouted_f, rerouted_b = pl.pallas_call(
        extras_kernel,
        out_shape=[thin, thin],
        in_specs=[free, smem] + [vmem] * 5,
        out_specs=[vmem] * 2,
        compiler_params=params,
        cost_estimate=pl.CostEstimate(
            flops=8 * 16 * width * depth, bytes_accessed=6 * 2**20, transcendentals=0
        ),
        name="extras",
    )(own, at, *extras, gain, *weights)
    shard_out = jax.ShapeDtypeStruct((1, depth, BLOCK), F32)
    grad_down, grad_up = pl.pallas_call(
        finish_kernel,
        out_shape=[shard_out, shard_out],
        in_specs=[vmem] * 2,
        out_specs=[vmem] * 2,
        compiler_params=params,
        cost_estimate=quick,
        name="finish",
    )(own, other)
    return (
        forward_out[None, None],
        backward_out[None, None],
        rerouted_f[None, :share],
        rerouted_b[None, :share],
        grad_down,
        grad_up,
    )


def solution(mesh):
    return jax.shard_map(
        body,
        mesh=mesh,
        in_specs=(
            P("section", "dp", None, None),
            P("section", "dp", None, None),
            P("section", None),
            P("section", None, "dp"),
            P("section", None, "dp"),
            P(),
            P(),
        ),
        out_specs=(
            P("section", "dp", None, None),
            P("section", "dp", None, None),
            P("section", "dp", None),
            P("section", "dp", None),
            P("section", None, "dp"),
            P("section", None, "dp"),
        ),
        check_vma=False,
    )
```

```python
import jax
import jax.numpy as jnp
from jax import lax
from jax.experimental import pallas as pl
from jax.experimental.pallas import tpu as pltpu
from jax.sharding import PartitionSpec as P

eps = 1e-05
N_Z = 8
N_DP = 32
BLOCK = 256
F32 = jnp.float32
BF16 = jnp.bfloat16


def place(y, z, c):
    return (y * N_Z + z) * 2 + c


PLACES = [(y, z, c) for y in range(2) for z in range(N_Z) for c in range(2)]
TO_CORE = [(place(y, z, c), place(y, z, 1 - c)) for y, z, c in PLACES]
TO_Y = [(place(y, z, c), place(1 - y, z, c)) for y, z, c in PLACES]
TO_UP = [(place(y, z, c), place(y, (z + 1) % N_Z, c)) for y, z, c in PLACES]
TO_DOWN = [(place(y, z, c), place(y, (z - 1) % N_Z, c)) for y, z, c in PLACES]
Z_GROUPS = [[place(y, z, c) for z in range(N_Z)] for y in range(2) for c in range(2)]


def over_dp(block, pairs):
    return lax.ppermute(block, "dp", pairs)


def over_section(block, distance):
    n = lax.axis_size("section")
    return lax.ppermute(block, "section", [(i, (i + distance) % n) for i in range(n)])


def over_both(block, distance, across):
    n = lax.axis_size("section")
    pairs = [
        (i * N_DP + place(y, z, c), (i + distance) % n * N_DP + place(y ^ across, z, c))
        for i in range(n)
        for y, z, c in PLACES
    ]
    return lax.ppermute(block, ("section", "dp"), pairs)


SLOTS = (4, 3, 5, 2, 6, 1, 7, 0)
N_FIRST = 3


def both_kernel(token, mine, other, out):
    out[0] = mine[...]
    out[1] = other[...]


def columns_of(refs, at, c, k, y):
    return refs[c].at[lax.rem(at[32] + k, N_Z), y]


def spot_of(c, k, y):
    return (c * N_Z + k) * 2 + y


def wide(ref):
    return ref[...].astype(F32)


def later_kernel(token, a_ref, out_ref):
    out_ref[...] = a_ref[...]


def open_kernel(keep, crossed, up, down):
    total = keep[0] + wide(crossed)[0]
    up[...] = total[:1].astype(BF16)
    down[...] = total[1:].astype(BF16)


def fold_kernel(token, keep_up, keep_down, cross_up, cross_down, got_up, got_down, up, down):
    top = keep_up[0] + wide(cross_up)[0]
    low = keep_down[0] + wide(cross_down)[0]
    if got_up.shape[0] == 1:
        up[0] = (top[0] + wide(got_up)[0]).astype(BF16)
        up[1] = top[1].astype(BF16)
        down[0] = low[0].astype(BF16)
        down[1] = (low[1] + wide(got_down)[0]).astype(BF16)
    else:
        up[...] = (top + wide(got_up)).astype(BF16)
        down[...] = (low + wide(got_down)).astype(BF16)


def close_kernel(token_1, token_2, keep, crossed, got_up, got_down, own, other):
    total = (keep[0] + wide(crossed)[0]) + (wide(got_up) + wide(got_down))
    own[...] = total[0]
    other[...] = total[1].astype(BF16)


def finish_kernel(own, got, grad_down, grad_up):
    total = (own[...] + wide(got)) * (1.0 / N_DP)
    grad_down[0] = total[0]
    grad_up[0] = total[1]


def square_sums(x_ref):
    rows, width = x_ref.shape

    def square(i, total):
        part = x_ref[:, pl.ds(pl.multiple_of(i * 512, 512), 512)].astype(F32)
        part = part * part
        return total + ((part[:, :128] + part[:, 128:256]) + (part[:, 256:384] + part[:, 384:]))

    total = lax.fori_loop(0, width // 512, square, jnp.zeros((rows, 128), F32))
    return lax.rsqrt(jnp.sum(total, axis=1, keepdims=True) * (1.0 / width) + eps)


def scale_kernel(x_ref, g_ref, inv_ref):
    inv_ref[...] = jnp.broadcast_to(square_sums(x_ref), inv_ref.shape)


def add_kernel(a_ref, b_ref, out_ref):
    out_ref[...] = a_ref[...] + b_ref[...]


def lows_of(at, x_ref, g_ref, gain_ref, w_refs, inv, normed):
    trans = (((1,), (1,)), ((), ()))
    low = back = None
    for c in range(2):
        for k in range(N_Z):
            for y in range(2):
                spot = spot_of(c, k, y)
                here = pl.ds(pl.multiple_of(at[spot], BLOCK), BLOCK)
                norm = (x_ref[:, here].astype(F32) * inv * gain_ref[:, here]).astype(BF16)
                if normed is not None:
                    normed[spot] = norm
                w = columns_of(w_refs, at, c, k, y)
                one = lax.dot_general(norm, w[0], trans, preferred_element_type=F32)
                two = lax.dot_general(g_ref[:, here], w[1], trans, preferred_element_type=F32)
                low, back = (one, two) if low is None else (low + one, back + two)
    return low, back


def terms_kernel(token, at, x_ref, g_ref, gain_ref, *refs):
    w_refs = refs[:2]
    inv_ref, keep_ref, first_ref, second_ref, low_ref, back_ref, dot_ref, normed = refs[2:]
    inv = inv_ref[:, :1]
    low, back = lows_of(at, x_ref, g_ref, gain_ref, w_refs, inv, normed)
    low16, back16 = low.astype(BF16), back.astype(BF16)
    low_ref[...] = low16
    back_ref[...] = back16
    dots = jnp.sum(back16.astype(F32) * low, axis=1, keepdims=True)
    dot_ref[...] = jnp.broadcast_to(dots, dot_ref.shape)
    low_t, back_t = low16.T, back16.T

    def term(spot):
        here = pl.ds(pl.multiple_of(at[spot], BLOCK), BLOCK)
        down = jnp.dot(back_t, normed[spot], preferred_element_type=F32)
        up = jnp.dot(low_t, g_ref[:, here], preferred_element_type=F32)
        return down, up

    for i, k in enumerate(SLOTS):
        out_ref, j = (first_ref, i) if i < N_FIRST else (second_ref, i - N_FIRST)
        for y in range(2):
            for which, value in enumerate(term(spot_of(1, k, y))):
                out_ref[j, y, which] = value.astype(BF16)
            for which, value in enumerate(term(spot_of(0, k, y))):
                keep_ref[i, y, which] = value


def write_outputs(at, x_ref, g_ref, gain_ref, w_refs, low, back, inv, slope, fwd, bwd, keeps=None):
    for c in range(2):
        for k in range(N_Z):
            for y in range(2):
                here = pl.ds(pl.multiple_of(at[spot_of(c, k, y)], BLOCK), BLOCK)
                w = columns_of(w_refs, at, c, k, y)
                lifted = jnp.dot(low, w[1], preferred_element_type=F32)
                pulled = jnp.dot(back, w[0], preferred_element_type=F32)
                part = x_ref[:, here].astype(F32)
                out = (part + lifted).astype(BF16)
                grad = g_ref[:, here].astype(F32) + (pulled * gain_ref[:, here] * inv - part * slope)
                grad = grad.astype(BF16)
                if keeps is not None:
                    out = jnp.where(keeps, out, jnp.zeros_like(out))
                    grad = jnp.where(keeps, grad, jnp.zeros_like(grad))
                fwd[:, here] = out
                bwd[:, here] = grad


def outputs_kernel(token, at, x_ref, g_ref, gain_ref, *refs):
    w_refs = refs[:2]
    low_ref, back_ref, inv_ref, dot_ref, fwd, bwd, mark = refs[2:]
    mark[...] = jnp.zeros_like(mark)
    inv = inv_ref[:, :1]
    slope = inv * inv * dot_ref[:, :1] * (1.0 / x_ref.shape[1])
    write_outputs(
        at, x_ref, g_ref, gain_ref, w_refs, low_ref[...], back_ref[...], inv, slope, fwd, bwd,
        at[33] == 1,
    )


def extras_kernel(token, at, x_ref, g_ref, gain_ref, *refs):
    w_refs = refs[:2]
    fwd, bwd = refs[2:]
    inv = square_sums(x_ref)
    low, back = lows_of(at, x_ref, g_ref, gain_ref, w_refs, inv, None)
    low16, back16 = low.astype(BF16), back.astype(BF16)
    dots = jnp.sum(back16.astype(F32) * low, axis=1, keepdims=True)
    slope = inv * inv * dots * (1.0 / x_ref.shape[1])
    write_outputs(at, x_ref, g_ref, gain_ref, w_refs, low16, back16, inv, slope, fwd, bwd)


def picks_kernel(who, failed, route, x_ref, g_ref, keep_ref, send_ref, pick):
    count = x_ref.shape[0]
    share = count // N_DP
    rank, section = who[0], who[1]
    y, c = rank // 16, rank % 2
    after, before = lax.rem(section + 1, 8), lax.rem(section + 7, 8)

    @pl.when(pl.program_id(0) == 0)
    def _():
        column = lax.broadcasted_iota(jnp.int32, (8, count), 1)
        line = lax.broadcasted_iota(jnp.int32, (8, count), 0)
        has_x = jnp.where(failed[after] == rank, 1.0, 0.0)
        has_g = jnp.where(failed[before] == rank, 1.0, 0.0)
        for c_rel in range(2):
            parts_x, parts_g = [], []
            for k in range(N_Z):
                for y_to in (y, 1 - y):
                    to = place(y_to, k, c if c_rel == 0 else 1 - c)
                    hit_x = (column == route[after, to] * share + line) & (line < share)
                    hit_g = (column == route[before, to] * share + line - share) & (line >= share)
                    parts_x.append(jnp.where(hit_x, has_x, 0.0))
                    parts_g.append(jnp.where(hit_g, has_g, 0.0))
            pick[c_rel, 0] = jnp.concatenate(parts_x, axis=0).astype(BF16)
            pick[c_rel, 1] = jnp.concatenate(parts_g, axis=0).astype(BF16)

    for c_rel, out_ref in ((0, keep_ref), (1, send_ref)):
        moved = jnp.dot(pick[c_rel, 0], x_ref[...], preferred_element_type=F32)
        moved += jnp.dot(pick[c_rel, 1], g_ref[...], preferred_element_type=F32)
        out_ref[...] = moved.astype(BF16)


def body(arriving, returning, gain, section_down_weight, section_up_weight, failed, route):
    section = lax.axis_index("section")
    rank = lax.axis_index("dp")
    y, z, c = rank // 16, (rank // 2) % N_Z, rank % 2
    count, width = arriving.shape[2], arriving.shape[3]
    depth = section_down_weight.shape[1]
    share = count // N_DP

    inbound = over_section(arriving, 1)[0, 0]
    upstream = over_section(returning, -1)[0, 0]

    here_x, here_g = arriving[0, 0], returning[0, 0]
    who = jnp.where(jnp.arange(2) == 0, rank, section).astype(jnp.int32)
    i = jnp.arange(34)
    i_y, i_z, i_c = i % 2, i // 2 % N_Z, i // 16
    spots = place(y ^ i_y, (z + i_z) % N_Z, c ^ i_c) * BLOCK
    kept = (rank != failed[section]).astype(jnp.int32)
    at = jnp.where(i < 32, spots, jnp.where(i == 32, z, kept)).astype(jnp.int32)
    smem = pl.BlockSpec(memory_space=pltpu.SMEM)
    vmem = pl.BlockSpec(memory_space=pltpu.VMEM)
    whole = jax.ShapeDtypeStruct((count, width), BF16)
    quick = pl.CostEstimate(flops=2**18, bytes_accessed=2**20, transcendentals=0)
    params = pltpu.CompilerParams(vmem_limit_bytes=28 * 2**20)
    step = 1024
    block = pl.BlockSpec((count, step), lambda i: (0, i))
    moved = pl.pallas_call(
        picks_kernel,
        grid=(width // step,),
        out_shape=[whole, whole],
        in_specs=[smem] * 3 + [block] * 2,
        out_specs=[block] * 2,
        scratch_shapes=[pltpu.VMEM((2, 2, count, count), BF16)],
        compiler_params=pltpu.CompilerParams(vmem_limit_bytes=60 * 2**20),
        cost_estimate=pl.CostEstimate(flops=0, bytes_accessed=1024, transcendentals=0),
        name="picks",
    )(who, failed, route, here_x, here_g)
    crossed = over_dp(moved[1], TO_CORE)
    stat = jax.ShapeDtypeStruct((count, 128), F32)
    free = pl.BlockSpec(memory_space=pl.ANY)
    inv = pl.pallas_call(
        scale_kernel,
        out_shape=stat,
        in_specs=[vmem, free],
        out_specs=vmem,
        compiler_params=params,
        cost_estimate=pl.CostEstimate(
            flops=2 * count * width, bytes_accessed=50331648, transcendentals=0
        ),
        name="scale",
    )(inbound, upstream)
    shard = jnp.concatenate([section_down_weight, section_up_weight], axis=0)
    chunk = (2, 2, depth, BLOCK)
    both = pl.pallas_call(
        both_kernel,
        out_shape=jax.ShapeDtypeStruct(chunk, BF16),
        in_specs=[free, vmem, vmem],
        out_specs=vmem,
        compiler_params=params,
        cost_estimate=quick,
        name="both",
    )(moved[0], shard, over_dp(shard, TO_Y))
    mine = lax.all_gather(both, "dp", axis=0, axis_index_groups=Z_GROUPS, tiled=False)
    weights = [mine, over_dp(mine, TO_CORE)]

    added = pl.pallas_call(
        add_kernel,
        grid=(4,),
        out_shape=whole,
        in_specs=[pl.BlockSpec((count // 4, width), lambda i: (i, 0))] * 2,
        out_specs=pl.BlockSpec((count // 4, width), lambda i: (i, 0)),
        compiler_params=params,
        cost_estimate=pl.CostEstimate(
            flops=count * width, bytes_accessed=1024, transcendentals=0
        ),
        name="add",
    )(moved[0], crossed)
    rows = lax.psum_scatter(
        added, "dp", scatter_dimension=0, axis_index_groups=Z_GROUPS, tiled=True
    )


    small = jax.ShapeDtypeStruct((count, depth), BF16)
    keep, first, second, low, back, dots = pl.pallas_call(
        terms_kernel,
        out_shape=[
            jax.ShapeDtypeStruct((N_Z, *chunk), F32),
            jax.ShapeDtypeStruct((N_FIRST, *chunk), BF16),
            jax.ShapeDtypeStruct((N_Z - N_FIRST, *chunk), BF16),
            small,
            small,
            stat,
        ],
        in_specs=[free, smem] + [vmem] * 6,
        out_specs=[vmem] * 6,
        scratch_shapes=[pltpu.VMEM((32, count, BLOCK), BF16)],
        compiler_params=params,
        cost_estimate=pl.CostEstimate(
            flops=8 * count * width * depth, bytes_accessed=16 * 2**20, transcendentals=0
        ),
        name="terms",
    )(added, at, inbound, upstream, gain, *weights, inv)
    first = over_dp(first, TO_CORE)

    def slot(i):
        return pl.BlockSpec((1, *chunk), lambda j: (i, 0, 0, 0, 0))

    def all_of(shape):
        return pl.BlockSpec(shape, lambda j: (0,) * len(shape))

    half = jax.ShapeDtypeStruct((1, *chunk[1:]), BF16)
    full = jax.ShapeDtypeStruct(chunk, BF16)
    up, down = pl.pallas_call(
        open_kernel,
        grid=(1,),
        out_shape=[half, half],
        in_specs=[slot(0), slot(0)],
        out_specs=[all_of(half.shape)] * 2,
        compiler_params=params,
        cost_estimate=quick,
        name="open",
    )(keep, first)

    second = pl.pallas_call(
        later_kernel,
        out_shape=jax.ShapeDtypeStruct(second.shape, BF16),
        in_specs=[free, vmem],
        out_specs=vmem,
        compiler_params=params,
        cost_estimate=quick,
        name="later",
    )(up, second)
    second = over_dp(second, TO_CORE)

    def fold(token, i, crossed, j, up, down):
        return pl.pallas_call(
            fold_kernel,
            grid=(1,),
            out_shape=[full, full],
            in_specs=[free, slot(i), slot(i + 1), slot(j), slot(j + 1)] + [all_of(up.shape)] * 2,
            out_specs=[all_of(full.shape)] * 2,
            compiler_params=params,
        cost_estimate=quick,
            name="fold",
        )(token, keep, keep, crossed, crossed, up, down)

    up, down = over_dp(up, TO_UP), over_dp(down, TO_DOWN)
    up, down = fold(inv, 1, first, 1, up, down)
    forward_out, backward_out, mark = pl.pallas_call(
        outputs_kernel,
        out_shape=[whole, whole, jax.ShapeDtypeStruct((8, 128), F32)],
        in_specs=[free, smem] + [vmem] * 9,
        out_specs=[vmem] * 3,
        compiler_params=params,
        cost_estimate=pl.CostEstimate(
            flops=4 * count * width * depth, bytes_accessed=14 * 2**20, transcendentals=0
        ),
        name="outputs",
    )(up, at, inbound, upstream, gain, *weights, low, back, inv, dots)

    up, down = over_dp(up, TO_UP), over_dp(down, TO_DOWN)
    up, down = fold(mark, 3, second, 0, up, down)
    up, down = over_dp(up, TO_UP), over_dp(down, TO_DOWN)
    up, down = fold(inv, 5, second, 2, up, down)
    rows = pl.pallas_call(
        later_kernel,
        out_shape=jax.ShapeDtypeStruct(rows.shape, BF16),
        in_specs=[free, vmem],
        out_specs=vmem,
        compiler_params=params,
        cost_estimate=quick,
        name="wait",
    )(up, rows)
    extras = []
    for i, distance in ((0, 1), (1, -1)):
        near = over_both(rows[i * share : (i + 1) * share], distance, 0)
        far = over_both(rows[8 + i * share : 8 + (i + 1) * share], distance, 1)
        extras.append(jnp.pad(near + far, ((0, 16 - share), (0, 0))))
    up, down = over_dp(up, TO_UP), over_dp(down, TO_DOWN)
    own, other = pl.pallas_call(
        close_kernel,
        grid=(1,),
        out_shape=[
            jax.ShapeDtypeStruct(chunk[1:], F32),
            jax.ShapeDtypeStruct(chunk[1:], BF16),
        ],
        in_specs=[free, free, slot(7), slot(4)] + [all_of(chunk)] * 2,
        out_specs=[all_of(chunk[1:])] * 2,
        compiler_params=params,
        cost_estimate=quick,
        name="close",
    )(extras[0], extras[1], keep, second, up, down)
    other = over_dp(other, TO_Y)
    thin = jax.ShapeDtypeStruct((16, width), BF16)
    rerouted_f, rerouted_b = pl.pallas_call(
        extras_kernel,
        out_shape=[thin, thin],
        in_specs=[free, smem] + [vmem] * 5,
        out_specs=[vmem] * 2,
        compiler_params=params,
        cost_estimate=pl.CostEstimate(
            flops=8 * 16 * width * depth, bytes_accessed=6 * 2**20, transcendentals=0
        ),
        name="extras",
    )(own, at, *extras, gain, *weights)
    shard_out = jax.ShapeDtypeStruct((1, depth, BLOCK), F32)
    grad_down, grad_up = pl.pallas_call(
        finish_kernel,
        out_shape=[shard_out, shard_out],
        in_specs=[vmem] * 2,
        out_specs=[vmem] * 2,
        compiler_params=params,
        cost_estimate=quick,
        name="finish",
    )(own, other)
    return (
        forward_out[None, None],
        backward_out[None, None],
        rerouted_f[None, :share],
        rerouted_b[None, :share],
        grad_down,
        grad_up,
    )


def solution(mesh):
    return jax.shard_map(
        body,
        mesh=mesh,
        in_specs=(
            P("section", "dp", None, None),
            P("section", "dp", None, None),
            P("section", None),
            P("section", None, "dp"),
            P("section", None, "dp"),
            P(),
            P(),
        ),
        out_specs=(
            P("section", "dp", None, None),
            P("section", "dp", None, None),
            P("section", "dp", None),
            P("section", "dp", None),
            P("section", None, "dp"),
            P("section", None, "dp"),
        ),
        check_vma=False,
    )
```

```python
import jax
import jax.numpy as jnp
from jax import lax
from jax.experimental import pallas as pl
from jax.experimental.pallas import tpu as pltpu
from jax.sharding import PartitionSpec as P

eps = 1e-05
N_Z = 8
N_DP = 32
BLOCK = 256
F32 = jnp.float32
BF16 = jnp.bfloat16


def place(y, z, c):
    return (y * N_Z + z) * 2 + c


PLACES = [(y, z, c) for y in range(2) for z in range(N_Z) for c in range(2)]
TO_CORE = [(place(y, z, c), place(y, z, 1 - c)) for y, z, c in PLACES]
TO_Y = [(place(y, z, c), place(1 - y, z, c)) for y, z, c in PLACES]
TO_UP = [(place(y, z, c), place(y, (z + 1) % N_Z, c)) for y, z, c in PLACES]
TO_DOWN = [(place(y, z, c), place(y, (z - 1) % N_Z, c)) for y, z, c in PLACES]
Z_GROUPS = [[place(y, z, c) for z in range(N_Z)] for y in range(2) for c in range(2)]


def over_dp(block, pairs):
    return lax.ppermute(block, "dp", pairs)


def over_section(block, distance):
    n = lax.axis_size("section")
    return lax.ppermute(block, "section", [(i, (i + distance) % n) for i in range(n)])


def over_both(block, distance, across):
    n = lax.axis_size("section")
    pairs = [
        (i * N_DP + place(y, z, c), (i + distance) % n * N_DP + place(y ^ across, z, c))
        for i in range(n)
        for y, z, c in PLACES
    ]
    return lax.ppermute(block, ("section", "dp"), pairs)


SLOTS = (4, 3, 5, 2, 6, 1, 7, 0)
N_FIRST = 3


def pair_kernel(down, up, out):
    out[0] = down[0]
    out[1] = up[0]


def both_kernel(token, mine, other, out):
    out[0] = mine[...]
    out[1] = other[...]


def columns_of(refs, at, c, k, y):
    return refs[c].at[lax.rem(at[32] + k, N_Z), y]


def spot_of(c, k, y):
    return (c * N_Z + k) * 2 + y


def wide(ref):
    return ref[...].astype(F32)


def later_kernel(token, a_ref, out_ref):
    out_ref[...] = a_ref[...]


def open_kernel(keep, crossed, up, down):
    total = keep[0] + wide(crossed)[0]
    up[...] = total[:1].astype(BF16)
    down[...] = total[1:].astype(BF16)


def fold_kernel(token, keep_up, keep_down, cross_up, cross_down, got_up, got_down, up, down):
    top = keep_up[0] + wide(cross_up)[0]
    low = keep_down[0] + wide(cross_down)[0]
    if got_up.shape[0] == 1:
        up[0] = (top[0] + wide(got_up)[0]).astype(BF16)
        up[1] = top[1].astype(BF16)
        down[0] = low[0].astype(BF16)
        down[1] = (low[1] + wide(got_down)[0]).astype(BF16)
    else:
        up[...] = (top + wide(got_up)).astype(BF16)
        down[...] = (low + wide(got_down)).astype(BF16)


def close_kernel(token_1, token_2, keep, crossed, got_up, got_down, own, other):
    total = (keep[0] + wide(crossed)[0]) + (wide(got_up) + wide(got_down))
    own[...] = total[0]
    other[...] = total[1].astype(BF16)


def finish_kernel(own, got, grad_down, grad_up):
    total = (own[...] + wide(got)) * (1.0 / N_DP)
    grad_down[0] = total[0]
    grad_up[0] = total[1]


def square_sums(x_ref):
    rows, width = x_ref.shape

    def square(i, total):
        part = x_ref[:, pl.ds(pl.multiple_of(i * 512, 512), 512)].astype(F32)
        part = part * part
        return total + ((part[:, :128] + part[:, 128:256]) + (part[:, 256:384] + part[:, 384:]))

    total = lax.fori_loop(0, width // 512, square, jnp.zeros((rows, 128), F32))
    return lax.rsqrt(jnp.sum(total, axis=1, keepdims=True) * (1.0 / width) + eps)


def scale_kernel(x_ref, g_ref, inv_ref):
    inv_ref[...] = jnp.broadcast_to(square_sums(x_ref), inv_ref.shape)


def add_kernel(a_ref, b_ref, out_ref):
    out_ref[...] = a_ref[...] + b_ref[...]


def lows_of(at, x_ref, g_ref, gain_ref, w_refs, inv, normed):
    trans = (((1,), (1,)), ((), ()))
    low = back = None
    for c in range(2):
        for k in range(N_Z):
            for y in range(2):
                spot = spot_of(c, k, y)
                here = pl.ds(pl.multiple_of(at[spot], BLOCK), BLOCK)
                norm = (x_ref[:, here].astype(F32) * inv * gain_ref[:, here]).astype(BF16)
                if normed is not None:
                    normed[spot] = norm
                w = columns_of(w_refs, at, c, k, y)
                one = lax.dot_general(norm, w[0], trans, preferred_element_type=F32)
                two = lax.dot_general(g_ref[:, here], w[1], trans, preferred_element_type=F32)
                low, back = (one, two) if low is None else (low + one, back + two)
    return low, back


def terms_kernel(token, at, x_ref, g_ref, gain_ref, *refs):
    w_refs = refs[:2]
    inv_ref, keep_ref, first_ref, second_ref, low_ref, back_ref, dot_ref, normed = refs[2:]
    inv = inv_ref[:, :1]
    low, back = lows_of(at, x_ref, g_ref, gain_ref, w_refs, inv, normed)
    low16, back16 = low.astype(BF16), back.astype(BF16)
    low_ref[...] = low16
    back_ref[...] = back16
    dots = jnp.sum(back16.astype(F32) * low, axis=1, keepdims=True)
    dot_ref[...] = jnp.broadcast_to(dots, dot_ref.shape)
    low_t, back_t = low16.T, back16.T

    def term(spot):
        here = pl.ds(pl.multiple_of(at[spot], BLOCK), BLOCK)
        down = jnp.dot(back_t, normed[spot], preferred_element_type=F32)
        up = jnp.dot(low_t, g_ref[:, here], preferred_element_type=F32)
        return down, up

    for i, k in enumerate(SLOTS):
        out_ref, j = (first_ref, i) if i < N_FIRST else (second_ref, i - N_FIRST)
        for y in range(2):
            for which, value in enumerate(term(spot_of(1, k, y))):
                out_ref[j, y, which] = value.astype(BF16)
            for which, value in enumerate(term(spot_of(0, k, y))):
                keep_ref[i, y, which] = value


def write_outputs(at, x_ref, g_ref, gain_ref, w_refs, low, back, inv, slope, fwd, bwd, keeps=None):
    for c in range(2):
        for k in range(N_Z):
            for y in range(2):
                here = pl.ds(pl.multiple_of(at[spot_of(c, k, y)], BLOCK), BLOCK)
                w = columns_of(w_refs, at, c, k, y)
                lifted = jnp.dot(low, w[1], preferred_element_type=F32)
                pulled = jnp.dot(back, w[0], preferred_element_type=F32)
                part = x_ref[:, here].astype(F32)
                out = (part + lifted).astype(BF16)
                grad = g_ref[:, here].astype(F32) + (pulled * gain_ref[:, here] * inv - part * slope)
                grad = grad.astype(BF16)
                if keeps is not None:
                    out = jnp.where(keeps, out, jnp.zeros_like(out))
                    grad = jnp.where(keeps, grad, jnp.zeros_like(grad))
                fwd[:, here] = out
                bwd[:, here] = grad


def outputs_kernel(token, at, x_ref, g_ref, gain_ref, *refs):
    w_refs = refs[:2]
    low_ref, back_ref, inv_ref, dot_ref, fwd, bwd, mark = refs[2:]
    mark[...] = jnp.zeros_like(mark)
    inv = inv_ref[:, :1]
    slope = inv * inv * dot_ref[:, :1] * (1.0 / x_ref.shape[1])
    write_outputs(
        at, x_ref, g_ref, gain_ref, w_refs, low_ref[...], back_ref[...], inv, slope, fwd, bwd,
        at[33] == 1,
    )


def extras_kernel(token, at, x_ref, g_ref, gain_ref, *refs):
    w_refs = refs[:2]
    fwd, bwd = refs[2:]
    inv = square_sums(x_ref)
    low, back = lows_of(at, x_ref, g_ref, gain_ref, w_refs, inv, None)
    low16, back16 = low.astype(BF16), back.astype(BF16)
    dots = jnp.sum(back16.astype(F32) * low, axis=1, keepdims=True)
    slope = inv * inv * dots * (1.0 / x_ref.shape[1])
    write_outputs(at, x_ref, g_ref, gain_ref, w_refs, low16, back16, inv, slope, fwd, bwd)


def picks_kernel(who, failed, route, x_ref, g_ref, keep_ref, send_ref, pick):
    count = x_ref.shape[0]
    share = count // N_DP
    rank, section = who[0], who[1]
    y, c = rank // 16, rank % 2
    after, before = lax.rem(section + 1, 8), lax.rem(section + 7, 8)

    @pl.when(pl.program_id(0) == 0)
    def _():
        column = lax.broadcasted_iota(jnp.int32, (8, count), 1)
        line = lax.broadcasted_iota(jnp.int32, (8, count), 0)
        has_x = jnp.where(failed[after] == rank, 1.0, 0.0)
        has_g = jnp.where(failed[before] == rank, 1.0, 0.0)
        for c_rel in range(2):
            parts_x, parts_g = [], []
            for k in range(N_Z):
                for y_to in (y, 1 - y):
                    to = place(y_to, k, c if c_rel == 0 else 1 - c)
                    hit_x = (column == route[after, to] * share + line) & (line < share)
                    hit_g = (column == route[before, to] * share + line - share) & (line >= share)
                    parts_x.append(jnp.where(hit_x, has_x, 0.0))
                    parts_g.append(jnp.where(hit_g, has_g, 0.0))
            here = pl.ds(c_rel * count, count)
            pick[here, :count] = jnp.concatenate(parts_x, axis=0).astype(BF16)
            pick[here, count:] = jnp.concatenate(parts_g, axis=0).astype(BF16)

    both = jnp.concatenate([x_ref[...], g_ref[...]], axis=0)
    moved = jnp.dot(pick[...], both, preferred_element_type=F32).astype(BF16)
    keep_ref[...] = moved[:count]
    send_ref[...] = moved[count:]


def body(arriving, returning, gain, section_down_weight, section_up_weight, failed, route):
    section = lax.axis_index("section")
    rank = lax.axis_index("dp")
    y, z, c = rank // 16, (rank // 2) % N_Z, rank % 2
    count, width = arriving.shape[2], arriving.shape[3]
    depth = section_down_weight.shape[1]
    share = count // N_DP

    inbound = over_section(arriving, 1)[0, 0]
    upstream = over_section(returning, -1)[0, 0]

    here_x, here_g = arriving[0, 0], returning[0, 0]
    who = jnp.where(jnp.arange(2) == 0, rank, section).astype(jnp.int32)
    i = jnp.arange(34)
    i_y, i_z, i_c = i % 2, i // 2 % N_Z, i // 16
    spots = place(y ^ i_y, (z + i_z) % N_Z, c ^ i_c) * BLOCK
    kept = (rank != failed[section]).astype(jnp.int32)
    at = jnp.where(i < 32, spots, jnp.where(i == 32, z, kept)).astype(jnp.int32)
    smem = pl.BlockSpec(memory_space=pltpu.SMEM)
    vmem = pl.BlockSpec(memory_space=pltpu.VMEM)
    whole = jax.ShapeDtypeStruct((count, width), BF16)
    quick = pl.CostEstimate(flops=2**18, bytes_accessed=2**20, transcendentals=0)
    params = pltpu.CompilerParams(vmem_limit_bytes=28 * 2**20)
    step = 1024
    block = pl.BlockSpec((count, step), lambda i: (0, i))
    moved = pl.pallas_call(
        picks_kernel,
        grid=(width // step,),
        out_shape=[whole, whole],
        in_specs=[smem] * 3 + [block] * 2,
        out_specs=[block] * 2,
        scratch_shapes=[pltpu.VMEM((2 * count, 2 * count), BF16)],
        compiler_params=pltpu.CompilerParams(vmem_limit_bytes=60 * 2**20),
        cost_estimate=pl.CostEstimate(flops=0, bytes_accessed=1024, transcendentals=0),
        name="picks",
    )(who, failed, route, here_x, here_g)
    crossed = over_dp(moved[1], TO_CORE)
    stat = jax.ShapeDtypeStruct((count, 128), F32)
    free = pl.BlockSpec(memory_space=pl.ANY)
    inv = pl.pallas_call(
        scale_kernel,
        out_shape=stat,
        in_specs=[vmem, free],
        out_specs=vmem,
        compiler_params=params,
        cost_estimate=pl.CostEstimate(
            flops=2 * count * width, bytes_accessed=50331648, transcendentals=0
        ),
        name="scale",
    )(inbound, upstream)
    shard = pl.pallas_call(
        pair_kernel,
        out_shape=jax.ShapeDtypeStruct((2, depth, BLOCK), BF16),
        in_specs=[vmem] * 2,
        out_specs=vmem,
        compiler_params=params,
        cost_estimate=quick,
        name="pair",
    )(section_down_weight, section_up_weight)
    chunk = (2, 2, depth, BLOCK)
    both = pl.pallas_call(
        both_kernel,
        out_shape=jax.ShapeDtypeStruct(chunk, BF16),
        in_specs=[free, vmem, vmem],
        out_specs=vmem,
        compiler_params=params,
        cost_estimate=quick,
        name="both",
    )(moved[0], shard, over_dp(shard, TO_Y))
    mine = lax.all_gather(both, "dp", axis=0, axis_index_groups=Z_GROUPS, tiled=False)
    weights = [mine, over_dp(mine, TO_CORE)]

    added = pl.pallas_call(
        add_kernel,
        grid=(4,),
        out_shape=whole,
        in_specs=[pl.BlockSpec((count // 4, width), lambda i: (i, 0))] * 2,
        out_specs=pl.BlockSpec((count // 4, width), lambda i: (i, 0)),
        compiler_params=params,
        cost_estimate=pl.CostEstimate(
            flops=count * width, bytes_accessed=1024, transcendentals=0
        ),
        name="add",
    )(moved[0], crossed)
    rows = lax.psum_scatter(
        added, "dp", scatter_dimension=0, axis_index_groups=Z_GROUPS, tiled=True
    )


    small = jax.ShapeDtypeStruct((count, depth), BF16)
    keep, first, second, low, back, dots = pl.pallas_call(
        terms_kernel,
        out_shape=[
            jax.ShapeDtypeStruct((N_Z, *chunk), F32),
            jax.ShapeDtypeStruct((N_FIRST, *chunk), BF16),
            jax.ShapeDtypeStruct((N_Z - N_FIRST, *chunk), BF16),
            small,
            small,
            stat,
        ],
        in_specs=[free, smem] + [vmem] * 6,
        out_specs=[vmem] * 6,
        scratch_shapes=[pltpu.VMEM((32, count, BLOCK), BF16)],
        compiler_params=params,
        cost_estimate=pl.CostEstimate(
            flops=8 * count * width * depth, bytes_accessed=16 * 2**20, transcendentals=0
        ),
        name="terms",
    )(added, at, inbound, upstream, gain, *weights, inv)
    first = over_dp(first, TO_CORE)

    def slot(i):
        return pl.BlockSpec((1, *chunk), lambda j: (i, 0, 0, 0, 0))

    def all_of(shape):
        return pl.BlockSpec(shape, lambda j: (0,) * len(shape))

    half = jax.ShapeDtypeStruct((1, *chunk[1:]), BF16)
    full = jax.ShapeDtypeStruct(chunk, BF16)
    up, down = pl.pallas_call(
        open_kernel,
        grid=(1,),
        out_shape=[half, half],
        in_specs=[slot(0), slot(0)],
        out_specs=[all_of(half.shape)] * 2,
        compiler_params=params,
        cost_estimate=quick,
        name="open",
    )(keep, first)

    second = pl.pallas_call(
        later_kernel,
        out_shape=jax.ShapeDtypeStruct(second.shape, BF16),
        in_specs=[free, vmem],
        out_specs=vmem,
        compiler_params=params,
        cost_estimate=quick,
        name="later",
    )(up, second)
    second = over_dp(second, TO_CORE)

    def fold(token, i, crossed, j, up, down):
        return pl.pallas_call(
            fold_kernel,
            grid=(1,),
            out_shape=[full, full],
            in_specs=[free, slot(i), slot(i + 1), slot(j), slot(j + 1)] + [all_of(up.shape)] * 2,
            out_specs=[all_of(full.shape)] * 2,
            compiler_params=params,
        cost_estimate=quick,
            name="fold",
        )(token, keep, keep, crossed, crossed, up, down)

    up, down = over_dp(up, TO_UP), over_dp(down, TO_DOWN)
    up, down = fold(inv, 1, first, 1, up, down)
    forward_out, backward_out, mark = pl.pallas_call(
        outputs_kernel,
        out_shape=[whole, whole, jax.ShapeDtypeStruct((8, 128), F32)],
        in_specs=[free, smem] + [vmem] * 9,
        out_specs=[vmem] * 3,
        compiler_params=params,
        cost_estimate=pl.CostEstimate(
            flops=4 * count * width * depth, bytes_accessed=14 * 2**20, transcendentals=0
        ),
        name="outputs",
    )(up, at, inbound, upstream, gain, *weights, low, back, inv, dots)

    up, down = over_dp(up, TO_UP), over_dp(down, TO_DOWN)
    up, down = fold(mark, 3, second, 0, up, down)
    up, down = over_dp(up, TO_UP), over_dp(down, TO_DOWN)
    up, down = fold(inv, 5, second, 2, up, down)
    rows = pl.pallas_call(
        later_kernel,
        out_shape=jax.ShapeDtypeStruct(rows.shape, BF16),
        in_specs=[free, vmem],
        out_specs=vmem,
        compiler_params=params,
        cost_estimate=quick,
        name="wait",
    )(up, rows)
    extras = []
    for i, distance in ((0, 1), (1, -1)):
        near = over_both(rows[i * share : (i + 1) * share], distance, 0)
        far = over_both(rows[8 + i * share : 8 + (i + 1) * share], distance, 1)
        extras.append(jnp.pad(near + far, ((0, 16 - share), (0, 0))))
    up, down = over_dp(up, TO_UP), over_dp(down, TO_DOWN)
    own, other = pl.pallas_call(
        close_kernel,
        grid=(1,),
        out_shape=[
            jax.ShapeDtypeStruct(chunk[1:], F32),
            jax.ShapeDtypeStruct(chunk[1:], BF16),
        ],
        in_specs=[free, free, slot(7), slot(4)] + [all_of(chunk)] * 2,
        out_specs=[all_of(chunk[1:])] * 2,
        compiler_params=params,
        cost_estimate=quick,
        name="close",
    )(extras[0], extras[1], keep, second, up, down)
    other = over_dp(other, TO_Y)
    thin = jax.ShapeDtypeStruct((16, width), BF16)
    rerouted_f, rerouted_b = pl.pallas_call(
        extras_kernel,
        out_shape=[thin, thin],
        in_specs=[free, smem] + [vmem] * 5,
        out_specs=[vmem] * 2,
        compiler_params=params,
        cost_estimate=pl.CostEstimate(
            flops=8 * 16 * width * depth, bytes_accessed=6 * 2**20, transcendentals=0
        ),
        name="extras",
    )(own, at, *extras, gain, *weights)
    shard_out = jax.ShapeDtypeStruct((1, depth, BLOCK), F32)
    grad_down, grad_up = pl.pallas_call(
        finish_kernel,
        out_shape=[shard_out, shard_out],
        in_specs=[vmem] * 2,
        out_specs=[vmem] * 2,
        compiler_params=params,
        cost_estimate=quick,
        name="finish",
    )(own, other)
    return (
        forward_out[None, None],
        backward_out[None, None],
        rerouted_f[None, :share],
        rerouted_b[None, :share],
        grad_down,
        grad_up,
    )


def solution(mesh):
    return jax.shard_map(
        body,
        mesh=mesh,
        in_specs=(
            P("section", "dp", None, None),
            P("section", "dp", None, None),
            P("section", None),
            P("section", None, "dp"),
            P("section", None, "dp"),
            P(),
            P(),
        ),
        out_specs=(
            P("section", "dp", None, None),
            P("section", "dp", None, None),
            P("section", "dp", None),
            P("section", "dp", None),
            P("section", None, "dp"),
            P("section", None, "dp"),
        ),
        check_vma=False,
    )
```
